512 devices in a mesh: dp: 32 (over z, y_hi, core), group: 16 (over y_lo, x).
Axes of the slice: x: 4, y: 8 (y_hi: 2, y_lo: 4; y = y_hi * 4 + y_lo), z: 8, core: 2. Of those that a mesh axis runs over, the one named last changes fastest.
Arguments:
- activations: bfloat16 [131072, 4096], P(('dp', 'group'))
- cotangent: bfloat16 [131072, 4096], P(('dp', 'group'))
- user_ids: int32 [512], P(('dp', 'group')), may hold values from 0 to 1, as said below
- adapters: bfloat16 [2, 2, 16, 4096], replicated, may hold values from -0.09375 to 0.09375
- clip_norm_ratio: float32 [1], replicated, may hold values from 3 to 5.5
Outputs:
- clipped_sum: float32 [2, 2, 16, 4096], P(None, None, None, 'group')
The draws below stay inside these ranges and needn't reach their ends.
Inputs may be any that keep to these rules, and one draw needn't show every extreme that they name: `user_ids`: each consecutive block of 16 sequences is one user group in which every user number names exactly 8 sequences.
All inputs are finite; a program needn't handle non-finite values.
Results may differ from the reference program's by a relative error of at most 0.0021.
Values sent between devices are 32-bit elements; how exact they have to be, the bound alone decides.
No kernel may reach another device: no remote copies, remote signals or barrier semaphores. Data moves between devices by JAX's collectives and lax.ppermute only.
A program may use at most 64 MiB of HBM per device.

```python
import math
import jax
import jax.numpy as jnp
from jax import lax

MODEL_WIDTH = 4096
ADAPTER_RANK = 16
SEQUENCE_LENGTH = 256
GROUP_USERS = 2
USER_SEQUENCES = 8
SEQS = 512
N_DP = 32


def owners_draw(key):
    group_seqs = USER_SEQUENCES * GROUP_USERS
    keys = jax.random.split(jax.random.fold_in(key, 37), SEQS // group_seqs)
    orders = jax.vmap(lambda single: jax.random.permutation(single, group_seqs))(keys)
    return (orders // USER_SEQUENCES).reshape(SEQS).astype(jnp.int32)


def rows_draw(key, salt):
    group_seqs = USER_SEQUENCES * GROUP_USERS
    owners = owners_draw(key)
    own_key = jax.random.fold_in(key, salt)
    key_noise, key_column, key_seq, key_token, key_offset = jax.random.split(own_key, 5)
    array_shape = (SEQS, SEQUENCE_LENGTH, MODEL_WIDTH)
    noise = jax.random.normal(key_noise, array_shape, jnp.float32)
    offsets = 0.25 * jax.random.normal(key_offset, (SEQS // group_seqs * GROUP_USERS, MODEL_WIDTH), jnp.float32)
    group_index = jnp.arange(SEQS, dtype=jnp.int32) // group_seqs
    seq_offset = offsets[group_index * GROUP_USERS + owners]
    place = jnp.arange(MODEL_WIDTH, dtype=jnp.float32) / MODEL_WIDTH
    column = jnp.exp(0.5 * jnp.log(3.0) * place + jax.random.uniform(key_column, (MODEL_WIDTH,), jnp.float32, 0.0, jnp.log(10.0))) / 6.0
    sequence = jnp.exp(jax.random.uniform(key_seq, (SEQS, 1, 1), jnp.float32, jnp.log(0.3), jnp.log(3.0)))
    token = jnp.exp(jax.random.uniform(key_token, (SEQS, SEQUENCE_LENGTH, 1), jnp.float32, jnp.log(0.5), jnp.log(2.0)))
    values = (noise + seq_offset[:, None, :]) * column[None, None, :] * sequence * token
    return values.reshape(SEQS * SEQUENCE_LENGTH, MODEL_WIDTH).astype(jnp.bfloat16)


def draw_activations(key, part):
    return rows_draw(key, 11)


def draw_cotangent(key, part):
    return rows_draw(key, 23)


def draw_user_ids(key, part):
    return owners_draw(key)


def scatter_about(key, dims, spread, reach, kind=jnp.bfloat16):
    return jnp.clip(spread * jax.random.normal(key, dims, jnp.float32), -reach, reach).astype(kind)


def setup_inputs(seed: int = 0) -> dict:
    splits = jax.random.split(jax.random.key(seed), 6)
    activations = draw_activations(jax.random.fold_in(splits[5], 71), 0)
    cotangent = draw_cotangent(jax.random.fold_in(splits[5], 71), 0)
    user_ids = draw_user_ids(jax.random.fold_in(splits[5], 71), 0)
    adapters = scatter_about(splits[3], (2, 2, ADAPTER_RANK, MODEL_WIDTH), MODEL_WIDTH ** -0.5, 0.09375)
    clip_norm_ratio = jnp.clip(jax.random.uniform(splits[4], (1,), jnp.float32, 3.0, 5.5), 3.0, 5.5)
    return {"activations": activations, "cotangent": cotangent, "user_ids": user_ids, "adapters": adapters, "clip_norm_ratio": clip_norm_ratio}


adapter_scale = 2.0

def project(input_batch, matrix):
    return jnp.einsum('td,rd->tr', input_batch.astype(jnp.float32), matrix.astype(jnp.float32))

def expand_rows(small_matrix, matrix):
    return jnp.dot(small_matrix, matrix, preferred_element_type=jnp.float32)

def user_grads(small_matrix, input_batch, token_owner):
    count = small_matrix.shape[0]
    masked = (small_matrix[:, None, :] * token_owner[:, :, None]).reshape(count, GROUP_USERS * small_matrix.shape[1])
    summed_gradient = jnp.einsum('tk,td->kd', masked.astype(jnp.float32), input_batch.astype(jnp.float32))
    return (adapter_scale * summed_gradient).reshape(GROUP_USERS, small_matrix.shape[1], input_batch.shape[1])

def reference(activations, cotangent, user_ids, adapters, clip_norm_ratio):
    group_seqs = USER_SEQUENCES * GROUP_USERS
    group_rows = group_seqs * SEQUENCE_LENGTH
    acts = activations.reshape(N_DP, group_rows, MODEL_WIDTH)
    cots = cotangent.reshape(N_DP, group_rows, MODEL_WIDTH)
    owners = user_ids.reshape(N_DP, group_seqs)
    clip_bound = clip_norm_ratio[0] * adapter_scale * math.sqrt(4 * ADAPTER_RANK * MODEL_WIDTH * USER_SEQUENCES * SEQUENCE_LENGTH)
    down_first = adapters[0, 0]
    first_up_weight = adapters[0, 1]
    second_down_weight = adapters[1, 0]
    up_second = adapters[1, 1]

    def one_group(items):
        input_tokens, backward_pass, owner = items
        seq_owner = (owner[:, None] == jnp.arange(GROUP_USERS, dtype=jnp.int32)[None, :]).astype(jnp.bfloat16)
        token_owner = jnp.broadcast_to(seq_owner[:, None, :], (group_seqs, SEQUENCE_LENGTH, GROUP_USERS)).reshape(group_rows, GROUP_USERS)
        first_inner_state = project(input_tokens, down_first).astype(jnp.bfloat16)
        hidden_state = (input_tokens.astype(jnp.float32) + adapter_scale * expand_rows(first_inner_state, first_up_weight)).astype(jnp.bfloat16)
        inner_second = project(hidden_state, second_down_weight).astype(jnp.bfloat16)
        second_cotangent = project(backward_pass, up_second).astype(jnp.bfloat16)
        hidden_cotangent = (backward_pass.astype(jnp.float32) + adapter_scale * expand_rows(second_cotangent, second_down_weight)).astype(jnp.bfloat16)
        back_first = project(hidden_cotangent, first_up_weight).astype(jnp.bfloat16)
        grads_first = jnp.stack([user_grads(back_first, input_tokens, token_owner), user_grads(first_inner_state, hidden_cotangent, token_owner)], axis=1)
        grads_second = jnp.stack([user_grads(second_cotangent, hidden_state, token_owner), user_grads(inner_second, backward_pass, token_owner)], axis=1)
        stacked = jnp.stack([grads_first, grads_second], axis=1)
        squares = lax.optimization_barrier(jnp.sum(stacked * stacked, axis=(1, 2, 3, 4)))
        norms = jnp.sqrt(squares)
        factor = clip_bound / jnp.maximum(norms, clip_bound)
        return lax.optimization_barrier(jnp.sum(factor[:, None, None, None, None] * stacked, axis=0))
    group_totals = lax.map(one_group, (acts, cots, owners))
    return lax.optimization_barrier(jnp.sum(group_totals, axis=0)) / (adapter_scale * math.sqrt(USER_SEQUENCES * SEQUENCE_LENGTH * GROUP_USERS * N_DP))
```

```python
import math

import jax
import jax.numpy as jnp
from jax import lax
from jax.experimental import pallas as pl
from jax.experimental.pallas import tpu as pltpu
from jax.sharding import Mesh, PartitionSpec as P

GROUP_USERS = 2
SCALE = 2.0
RANK = 16
WIDTH = 4096
TOKENS = 256
PEERS = 16
SLICE = WIDTH // PEERS
LANES = 128
ROWS = 4 * RANK * SLICE // LANES
SENT = ROWS + 8
USER_TOKENS = 8 * 256
N_DP = 32
CHUNK = 512

DP = ("z", "y_hi", "core")
GROUP = ("y_lo", "x")
VMEM = pl.BlockSpec(memory_space=pltpu.VMEM)
SMEM = pl.BlockSpec(memory_space=pltpu.SMEM)
F32 = jnp.float32
BF16 = jnp.bfloat16


def nt(a, b, precision=None):
    return lax.dot_general(
        a, b, (((1,), (1,)), ((), ())), preferred_element_type=F32, precision=precision
    )


def nn(a, b, precision=None):
    return jnp.dot(a, b, preferred_element_type=F32, precision=precision)


def gradient_kernel(x_ref, c_ref, adapters_ref, user_ref, out_ref):
    down1, up1 = adapters_ref[0, 0], adapters_ref[0, 1]
    down2, up2 = adapters_ref[1, 0], adapters_ref[1, 1]
    exact = lax.Precision.HIGHEST
    mixed = nt(down2, up1)
    from_x = nt(jnp.concatenate([down1, down2], axis=0), x_ref[...])
    from_c = nt(jnp.concatenate([up2, up1], axis=0), c_ref[...])
    z1 = from_x[:RANK].astype(BF16)
    q2 = from_c[:RANK].astype(BF16)
    z2 = (from_x[RANK:] + SCALE * nn(mixed, z1.astype(F32), exact)).astype(BF16)
    mixed_t = nt(up1, down2)
    q1 = (from_c[RANK:] + SCALE * nn(mixed_t, q2.astype(F32), exact)).astype(BF16)
    cross = (SCALE * SCALE) * nt(q2, z1)
    cross_t = (SCALE * SCALE) * nt(z1, q2)

    def split(value):
        high = value.astype(BF16)
        return jnp.concatenate([high, (value - high.astype(F32)).astype(BF16)], axis=0)

    cross2, cross2_t = split(cross), split(cross_t)
    left_x = jnp.concatenate([q1, q2], axis=0)
    left_c = jnp.concatenate([z1, z2], axis=0)
    for peer in range(PEERS):
        columns = pl.ds(peer * SLICE, SLICE)
        to_x = SCALE * nn(left_x, x_ref[:, columns])
        to_c = SCALE * nn(left_c, c_ref[:, columns])
        add_a2 = nn(cross2, adapters_ref[0, 1, :, columns])
        add_b1 = nn(cross2_t, adapters_ref[1, 0, :, columns])
        terms = (
            to_x[:RANK],
            to_c[:RANK] + (add_b1[:RANK] + add_b1[RANK:]),
            to_x[RANK:] + (add_a2[:RANK] + add_a2[RANK:]),
            to_c[RANK:],
        )
        for half in range(SLICE // LANES):
            for k, term in enumerate(terms):
                at = half * 4 * RANK + k * RANK
                out_ref[peer, at : at + RANK, :] = term[:, half * LANES : (half + 1) * LANES]
        out_ref[peer, ROWS:, :] = jnp.full((SENT - ROWS, LANES), user_ref[0].astype(F32), F32)


def users_kernel(got_ref, sums_ref, squares_ref):
    sums = [jnp.zeros((ROWS, LANES), F32) for _ in range(GROUP_USERS)]
    for peer in range(PEERS):
        term = got_ref[peer, :ROWS, :]
        owner = got_ref[peer, ROWS : ROWS + 1, :]
        for user in range(GROUP_USERS):
            sums[user] += jnp.where(owner == float(user), term, 0.0)
    for user in range(GROUP_USERS):
        sums_ref[user] = sums[user]
        total = jnp.sum(jnp.sum(sums[user] * sums[user], axis=0, keepdims=True), axis=1, keepdims=True)
        squares_ref[:, user, :] = jnp.broadcast_to(total, (PEERS, LANES))


def clip_kernel(ratio_ref, squares_ref, sums_ref, out_ref):
    bound = ratio_ref[0] * (SCALE * math.sqrt(4 * RANK * WIDTH * USER_TOKENS))
    squares = jnp.sum(squares_ref[...], axis=0)
    factor = bound / jnp.maximum(jnp.sqrt(squares), bound)
    total = factor[0:1] * sums_ref[0]
    for user in range(1, GROUP_USERS):
        total += factor[user : user + 1] * sums_ref[user]
    out_ref[...] = total


def on_device(activations, cotangent, user_ids, adapters, clip_norm_ratio):
    params = pltpu.CompilerParams(vmem_limit_bytes=40 * 1024 * 1024)
    terms = pl.pallas_call(
        gradient_kernel,
        out_shape=jax.ShapeDtypeStruct((PEERS, SENT, LANES), F32),
        in_specs=[VMEM, VMEM, VMEM, SMEM],
        out_specs=VMEM,
        compiler_params=params,
    )(activations, cotangent, adapters, user_ids)
    got = lax.all_to_all(terms, GROUP, 0, 0, tiled=True)
    sums, squares = pl.pallas_call(
        users_kernel,
        out_shape=(
            jax.ShapeDtypeStruct((GROUP_USERS, ROWS, LANES), F32),
            jax.ShapeDtypeStruct((PEERS, GROUP_USERS, LANES), F32),
        ),
        in_specs=[VMEM],
        out_specs=(VMEM, VMEM),
        compiler_params=params,
    )(got)
    squares = lax.all_to_all(squares, GROUP, 0, 0, tiled=True)
    total = pl.pallas_call(
        clip_kernel,
        out_shape=jax.ShapeDtypeStruct((ROWS, LANES), F32),
        in_specs=[SMEM, VMEM, VMEM],
        out_specs=VMEM,
        compiler_params=params,
    )(clip_norm_ratio, squares, sums)
    total += lax.ppermute(total, "core", [(0, 1), (1, 0)])
    total += lax.ppermute(total, "y_hi", [(0, 1), (1, 0)])
    ring = lax.axis_size("z")
    parts = lax.all_to_all(jnp.broadcast_to(total[None], (ring, ROWS, LANES)), "z", 0, 0, tiled=True)
    total = jnp.sum(parts, axis=0) / (SCALE * math.sqrt(USER_TOKENS * GROUP_USERS * N_DP))
    total = total.reshape(SLICE // LANES, 2, 2, RANK, LANES)
    return total.transpose(1, 2, 3, 0, 4).reshape(2, 2, RANK, SLICE)


def solution(mesh):
    fine = Mesh(mesh.devices.reshape(8, 2, 2, 4, 4), DP + GROUP)
    rows = P(DP + GROUP)
    return jax.shard_map(
        on_device,
        mesh=fine,
        in_specs=(rows, rows, rows, P(), P()),
        out_specs=P(None, None, None, GROUP),
        check_vma=False,
    )
```

```python
import math

import jax
import jax.numpy as jnp
from jax import lax
from jax.experimental import pallas as pl
from jax.experimental.pallas import tpu as pltpu
from jax.sharding import Mesh, PartitionSpec as P

GROUP_USERS = 2
SCALE = 2.0
RANK = 16
WIDTH = 4096
TOKENS = 256
PEERS = 16
SLICE = WIDTH // PEERS
LANES = 128
HALF = 4 * RANK
ROWS = HALF * SLICE // LANES
SENT = ROWS + 8
USER_TOKENS = 8 * 256
N_DP = 32
PARTS = 4
PART = WIDTH // PARTS
RING = 8

DP = ("z", "y_hi", "core")
GROUP = ("y_lo", "x")
VMEM = pl.BlockSpec(memory_space=pltpu.VMEM)
SMEM = pl.BlockSpec(memory_space=pltpu.SMEM)
HBM = pl.BlockSpec(memory_space=pltpu.HBM)
F32 = jnp.float32
BF16 = jnp.bfloat16
PARAMS = pltpu.CompilerParams(vmem_limit_bytes=40 * 1024 * 1024)
WIDE = pltpu.CompilerParams(vmem_limit_bytes=60 * 1024 * 1024)


def shape(*dims):
    return jax.ShapeDtypeStruct(dims, F32)


def nt(a, b, precision=None):
    return lax.dot_general(
        a, b, (((1,), (1,)), ((), ())), preferred_element_type=F32, precision=precision
    )


def nn(a, b, precision=None):
    return jnp.dot(a, b, preferred_element_type=F32, precision=precision)


def split(value):
    high = value.astype(BF16)
    return jnp.concatenate([high, (value - high.astype(F32)).astype(BF16)], axis=0)


def halves(value):
    return value[:RANK] + value[RANK:]


def gradient_kernel(
    x_hbm, c_hbm, adapters_hbm, user_ref, out_hbm, x_ref, c_ref, adapters_ref, out_ref, sems, out_sems
):
    copies = []
    for part in range(PARTS):
        at = pl.ds(part * PART, PART)
        copies.append(
            (
                pltpu.make_async_copy(adapters_hbm.at[:, :, :, at], adapters_ref.at[:, :, :, at], sems.at[0, part]),
                pltpu.make_async_copy(x_hbm.at[:, at], x_ref.at[:, at], sems.at[1, part]),
                pltpu.make_async_copy(c_hbm.at[:, at], c_ref.at[:, at], sems.at[2, part]),
            )
        )
    for group in copies:
        for copy in group:
            copy.start()
    from_x = jnp.zeros((2 * RANK, TOKENS), F32)
    from_c = jnp.zeros((2 * RANK, TOKENS), F32)
    mixed = jnp.zeros((RANK, RANK), F32)
    mixed_t = jnp.zeros((RANK, RANK), F32)
    for part in range(PARTS):
        for copy in copies[part]:
            copy.wait()
        at = pl.ds(part * PART, PART)
        down1, up1 = adapters_ref[0, 0, :, at], adapters_ref[0, 1, :, at]
        down2, up2 = adapters_ref[1, 0, :, at], adapters_ref[1, 1, :, at]
        from_x += nt(jnp.concatenate([down1, down2], axis=0), x_ref[:, at])
        from_c += nt(jnp.concatenate([up2, up1], axis=0), c_ref[:, at])
        mixed += nt(down2, up1)
        mixed_t += nt(up1, down2)
    exact = lax.Precision.HIGHEST
    z1 = from_x[:RANK].astype(BF16)
    q2 = from_c[:RANK].astype(BF16)
    z2 = (from_x[RANK:] + SCALE * nn(mixed, z1.astype(F32), exact)).astype(BF16)
    q1 = (from_c[RANK:] + SCALE * nn(mixed_t, q2.astype(F32), exact)).astype(BF16)
    cross = split((SCALE * SCALE) * nt(q2, z1))
    cross_t = split((SCALE * SCALE) * nt(z1, q2))
    left_x = jnp.concatenate([q1, q2], axis=0)
    left_c = jnp.concatenate([z1, z2], axis=0)
    sends = []
    for peer in range(PEERS):
        columns = pl.ds(peer * SLICE, SLICE)
        to_x = SCALE * nn(left_x, x_ref[:, columns])
        to_c = SCALE * nn(left_c, c_ref[:, columns])
        add_a2 = halves(nn(cross, adapters_ref[0, 1, :, columns]))
        add_b1 = halves(nn(cross_t, adapters_ref[1, 0, :, columns]))
        terms = (to_x[:RANK], to_c[:RANK] + add_b1, to_x[RANK:] + add_a2, to_c[RANK:])
        for half in range(SLICE // LANES):
            for k, term in enumerate(terms):
                at = half * HALF + k * RANK
                out_ref[peer, at : at + RANK, :] = term[:, half * LANES : (half + 1) * LANES]
        out_ref[peer, ROWS:, :] = jnp.full((SENT - ROWS, LANES), user_ref[0].astype(F32), F32)
        send = pltpu.make_async_copy(out_ref.at[peer], out_hbm.at[peer], out_sems.at[peer])
        send.start()
        sends.append(send)
    for send in sends:
        send.wait()


def users_kernel(got_ref, sums_ref, squares_ref):
    sums = [jnp.zeros((ROWS, LANES), F32) for _ in range(GROUP_USERS)]
    for peer in range(PEERS):
        term = got_ref[peer, :ROWS, :]
        owner = got_ref[peer, ROWS : ROWS + 1, :]
        for user in range(GROUP_USERS):
            sums[user] += jnp.where(owner == float(user), term, 0.0)
    for user in range(GROUP_USERS):
        sums_ref[user] = sums[user]
        square = jnp.sum(jnp.sum(sums[user] * sums[user], axis=0, keepdims=True), axis=1, keepdims=True)
        squares_ref[:, user, :] = jnp.broadcast_to(square, (PEERS, LANES))


def clip_kernel(ratio_ref, squares_ref, sums_ref, out_ref):
    bound = ratio_ref[0] * (SCALE * math.sqrt(4 * RANK * WIDTH * USER_TOKENS))
    squares = jnp.sum(squares_ref[...], axis=0)
    factor = bound / jnp.maximum(jnp.sqrt(squares), bound)
    total = factor[0:1] * sums_ref[0]
    for user in range(1, GROUP_USERS):
        total += factor[user : user + 1] * sums_ref[user]
    for half in range(SLICE // LANES):
        out_ref[half] = total[half * HALF : (half + 1) * HALF]


def chip_kernel(core_ref, pair_ref, out_ref):
    core = core_ref[0]
    out_ref[...] = pair_ref[0, core] + pair_ref[1, core]


def spread_kernel(pair_ref, out_ref):
    out_ref[...] = jnp.broadcast_to((pair_ref[0] + pair_ref[1])[None], (RING, HALF, LANES))


def total_kernel(parts_ref, out_ref):
    total = parts_ref[0]
    for part in range(1, RING):
        total += parts_ref[part]
    out_ref[...] = total / (SCALE * math.sqrt(USER_TOKENS * GROUP_USERS * N_DP))


def call(kernel, out_shape, *args, scalars=0):
    several = isinstance(out_shape, tuple)
    return pl.pallas_call(
        kernel,
        out_shape=out_shape,
        in_specs=[SMEM] * scalars + [VMEM] * (len(args) - scalars),
        out_specs=(VMEM,) * len(out_shape) if several else VMEM,
        compiler_params=PARAMS,
    )(*args)


def on_device(activations, cotangent, user_ids, adapters, clip_norm_ratio):
    terms = pl.pallas_call(
        gradient_kernel,
        out_shape=shape(PEERS, SENT, LANES),
        in_specs=[HBM, HBM, HBM, SMEM],
        out_specs=HBM,
        scratch_shapes=[
            pltpu.VMEM((TOKENS, WIDTH), BF16),
            pltpu.VMEM((TOKENS, WIDTH), BF16),
            pltpu.VMEM((2, 2, RANK, WIDTH), BF16),
            pltpu.VMEM((PEERS, SENT, LANES), F32),
            pltpu.SemaphoreType.DMA((3, PARTS)),
            pltpu.SemaphoreType.DMA((PEERS,)),
        ],
        compiler_params=WIDE,
    )(activations, cotangent, adapters, user_ids)
    terms = lax.all_to_all(terms, GROUP, 0, 0, tiled=True)
    sums, squares = call(
        users_kernel, (shape(GROUP_USERS, ROWS, LANES), shape(PEERS, GROUP_USERS, LANES)), terms
    )
    squares = lax.all_to_all(squares, GROUP, 0, 0, tiled=True)
    clipped = call(clip_kernel, shape(2, HALF, LANES), clip_norm_ratio, squares, sums, scalars=1)
    pair = lax.all_gather(clipped, "core")
    core = lax.axis_index("core")[None]
    chip = call(chip_kernel, shape(HALF, LANES), core, pair, scalars=1)
    parts = call(spread_kernel, shape(RING, HALF, LANES), lax.all_gather(chip, "y_hi"))
    parts = lax.all_to_all(parts, "z", 0, 0, tiled=True)
    total = call(total_kernel, shape(HALF, LANES), parts)
    total = lax.all_gather(total, "core", axis=1, tiled=True)
    return total.reshape(2, 2, RANK, SLICE)


def solution(mesh):
    fine = Mesh(mesh.devices.reshape(8, 2, 2, 4, 4), DP + GROUP)
    rows = P(DP + GROUP)
    return jax.shard_map(
        on_device,
        mesh=fine,
        in_specs=(rows, rows, rows, P(), P()),
        out_specs=P(None, None, None, GROUP),
        check_vma=False,
    )
```

```python
import math

import jax
import jax.numpy as jnp
from jax import lax
from jax.experimental import pallas as pl
from jax.experimental.pallas import tpu as pltpu
from jax.sharding import Mesh, PartitionSpec as P

GROUP_USERS = 2
SCALE = 2.0
RANK = 16
WIDTH = 4096
TOKENS = 256
NEAR = 8
FAR = 2
PEERS = NEAR * FAR
CORES = 2
SLICE = WIDTH // PEERS
LANES = 128
HALF = 4 * RANK
ROWS = HALF * SLICE // LANES
SENT = FAR * ROWS + 8
USER_TOKENS = 8 * 256
N_DP = 32
PARTS = 4
PART = WIDTH // PARTS
RING = 8

DP = ("z", "y_hi", "core")
GROUP = ("y_mid", "y_low", "x")
VMEM = pl.BlockSpec(memory_space=pltpu.VMEM)
SMEM = pl.BlockSpec(memory_space=pltpu.SMEM)
HBM = pl.BlockSpec(memory_space=pltpu.HBM)
F32 = jnp.float32
BF16 = jnp.bfloat16
PARAMS = pltpu.CompilerParams(vmem_limit_bytes=40 * 1024 * 1024)
WIDE = pltpu.CompilerParams(vmem_limit_bytes=60 * 1024 * 1024)


def shape(*dims):
    return jax.ShapeDtypeStruct(dims, F32)


def nt(a, b, precision=None):
    return lax.dot_general(
        a, b, (((1,), (1,)), ((), ())), preferred_element_type=F32, precision=precision
    )


def nn(a, b, precision=None):
    return jnp.dot(a, b, preferred_element_type=F32, precision=precision)


def split(value):
    high = value.astype(BF16)
    return jnp.concatenate([high, (value - high.astype(F32)).astype(BF16)], axis=0)


def halves(value):
    return value[:RANK] + value[RANK:]


def gradient_kernel(
    x_hbm, c_hbm, adapters_hbm, user_ref, out_hbm, x_ref, c_ref, adapters_ref, out_ref, sems, out_sems
):
    copies = []
    for part in range(PARTS):
        at = pl.ds(part * PART, PART)
        copies.append(
            (
                pltpu.make_async_copy(adapters_hbm.at[:, :, :, at], adapters_ref.at[:, :, :, at], sems.at[0, part]),
                pltpu.make_async_copy(x_hbm.at[:, at], x_ref.at[:, at], sems.at[1, part]),
                pltpu.make_async_copy(c_hbm.at[:, at], c_ref.at[:, at], sems.at[2, part]),
            )
        )
    for group in copies:
        for copy in group:
            copy.start()
    from_x = jnp.zeros((2 * RANK, TOKENS), F32)
    from_c = jnp.zeros((2 * RANK, TOKENS), F32)
    mixed = jnp.zeros((RANK, RANK), F32)
    mixed_t = jnp.zeros((RANK, RANK), F32)
    for part in range(PARTS):
        for copy in copies[part]:
            copy.wait()
        at = pl.ds(part * PART, PART)
        down1, up1 = adapters_ref[0, 0, :, at], adapters_ref[0, 1, :, at]
        down2, up2 = adapters_ref[1, 0, :, at], adapters_ref[1, 1, :, at]
        from_x += nt(jnp.concatenate([down1, down2], axis=0), x_ref[:, at])
        from_c += nt(jnp.concatenate([up2, up1], axis=0), c_ref[:, at])
        mixed += nt(down2, up1)
        mixed_t += nt(up1, down2)
    exact = lax.Precision.HIGHEST
    z1 = from_x[:RANK].astype(BF16)
    q2 = from_c[:RANK].astype(BF16)
    z2 = (from_x[RANK:] + SCALE * nn(mixed, z1.astype(F32), exact)).astype(BF16)
    q1 = (from_c[RANK:] + SCALE * nn(mixed_t, q2.astype(F32), exact)).astype(BF16)
    cross = split((SCALE * SCALE) * nt(q2, z1))
    cross_t = split((SCALE * SCALE) * nt(z1, q2))
    left_x = jnp.concatenate([q1, q2], axis=0)
    left_c = jnp.concatenate([z1, z2], axis=0)
    sends = []
    for near in range(NEAR):
        for far in range(FAR):
            columns = pl.ds((far * NEAR + near) * SLICE, SLICE)
            to_x = SCALE * nn(left_x, x_ref[:, columns])
            to_c = SCALE * nn(left_c, c_ref[:, columns])
            add_a2 = halves(nn(cross, adapters_ref[0, 1, :, columns]))
            add_b1 = halves(nn(cross_t, adapters_ref[1, 0, :, columns]))
            terms = (to_x[:RANK], to_c[:RANK] + add_b1, to_x[RANK:] + add_a2, to_c[RANK:])
            for half in range(SLICE // LANES):
                for k, term in enumerate(terms):
                    at = far * ROWS + half * HALF + k * RANK
                    out_ref[near, at : at + RANK, :] = term[:, half * LANES : (half + 1) * LANES]
        out_ref[near, FAR * ROWS :, :] = jnp.full((SENT - FAR * ROWS, LANES), user_ref[0].astype(F32), F32)
        send = pltpu.make_async_copy(out_ref.at[near], out_hbm.at[near], out_sems.at[near])
        send.start()
        sends.append(send)
    for send in sends:
        send.wait()


def users_kernel(mid_ref, got_ref, keep_ref, send_ref):
    mid = mid_ref[0]
    for far, out_ref in ((mid, keep_ref), (1 - mid, send_ref)):
        rows = pl.ds(pl.multiple_of(far * ROWS, ROWS), ROWS)
        sums = [jnp.zeros((ROWS, LANES), F32) for _ in range(GROUP_USERS)]
        for near in range(NEAR):
            term = got_ref[near, rows, :]
            owner = got_ref[near, FAR * ROWS : FAR * ROWS + 1, :]
            for user in range(GROUP_USERS):
                sums[user] += jnp.where(owner == float(user), term, 0.0)
        for user in range(GROUP_USERS):
            out_ref[user] = sums[user]


def squares_kernel(mid_ref, keep_ref, got_ref, sums_ref, squares_ref):
    partner = 1 - mid_ref[0]
    for user in range(GROUP_USERS):
        total = keep_ref[user] + got_ref[partner, user]
        sums_ref[user] = total
        square = jnp.sum(jnp.sum(total * total, axis=0, keepdims=True), axis=1, keepdims=True)
        squares_ref[:, user, :] = jnp.broadcast_to(square, (CORES * PEERS, LANES))


def clip_kernel(core_ref, ratio_ref, squares_ref, sums_ref, out_ref):
    rows = pl.ds(pl.multiple_of(core_ref[0] * HALF, HALF), HALF)
    bound = ratio_ref[0] * (SCALE * math.sqrt(4 * RANK * WIDTH * USER_TOKENS))
    total = jnp.zeros((HALF, LANES), F32)
    for core in range(CORES):
        squares = jnp.sum(squares_ref[core * PEERS : (core + 1) * PEERS], axis=0)
        factor = bound / jnp.maximum(jnp.sqrt(squares), bound)
        for user in range(GROUP_USERS):
            total += factor[user : user + 1] * sums_ref[core, user, rows, :]
    out_ref[...] = total


def spread_kernel(pair_ref, out_ref):
    out_ref[...] = jnp.broadcast_to((pair_ref[0] + pair_ref[1])[None], (RING, HALF, LANES))


def total_kernel(parts_ref, out_ref):
    total = parts_ref[0]
    for part in range(1, RING):
        total += parts_ref[part]
    out_ref[...] = total / (SCALE * math.sqrt(USER_TOKENS * GROUP_USERS * N_DP))


def call(kernel, out_shape, *args, scalars=0):
    several = isinstance(out_shape, tuple)
    return pl.pallas_call(
        kernel,
        out_shape=out_shape,
        in_specs=[SMEM] * scalars + [VMEM] * (len(args) - scalars),
        out_specs=(VMEM,) * len(out_shape) if several else VMEM,
        compiler_params=PARAMS,
    )(*args)


def on_device(activations, cotangent, user_ids, adapters, clip_norm_ratio):
    mid, core = lax.axis_index("y_mid")[None], lax.axis_index("core")[None]
    terms = pl.pallas_call(
        gradient_kernel,
        out_shape=shape(NEAR, SENT, LANES),
        in_specs=[HBM, HBM, HBM, SMEM],
        out_specs=HBM,
        scratch_shapes=[
            pltpu.VMEM((TOKENS, WIDTH), BF16),
            pltpu.VMEM((TOKENS, WIDTH), BF16),
            pltpu.VMEM((2, 2, RANK, WIDTH), BF16),
            pltpu.VMEM((NEAR, SENT, LANES), F32),
            pltpu.SemaphoreType.DMA((3, PARTS)),
            pltpu.SemaphoreType.DMA((NEAR,)),
        ],
        compiler_params=WIDE,
    )(activations, cotangent, adapters, user_ids)
    terms = lax.all_to_all(terms, ("y_low", "x"), 0, 0, tiled=True)
    users = shape(GROUP_USERS, ROWS, LANES)
    keep, send = call(users_kernel, (users, users), mid, terms, scalars=1)
    got = lax.all_gather(send, "y_mid")
    sums, squares = call(
        squares_kernel, (users, shape(CORES * PEERS, GROUP_USERS, LANES)), mid, keep, got, scalars=1
    )
    squares = lax.all_to_all(squares, ("core",) + GROUP, 0, 0, tiled=True)
    sums = lax.all_gather(sums, "core")
    chip = call(clip_kernel, shape(HALF, LANES), core, clip_norm_ratio, squares, sums, scalars=2)
    parts = call(spread_kernel, shape(RING, HALF, LANES), lax.all_gather(chip, "y_hi"))
    parts = lax.all_to_all(parts, "z", 0, 0, tiled=True)
    total = call(total_kernel, shape(HALF, LANES), parts)
    total = lax.all_gather(total, "core", axis=1, tiled=True)
    return total.reshape(2, 2, RANK, SLICE)


def solution(mesh):
    fine = Mesh(mesh.devices.reshape(8, 2, 2, 2, 2, 4), DP + GROUP)
    rows = P(DP + GROUP)
    return jax.shard_map(
        on_device,
        mesh=fine,
        in_specs=(rows, rows, rows, P(), P()),
        out_specs=P(None, None, None, GROUP),
        check_vma=False,
    )
```

```python
import math

import jax
import jax.numpy as jnp
from jax import lax
from jax.experimental import pallas as pl
from jax.experimental.pallas import tpu as pltpu
from jax.sharding import Mesh, PartitionSpec as P

GROUP_USERS = 2
SCALE = 2.0
RANK = 16
WIDTH = 4096
TOKENS = 256
NEAR = 8
NEAR_YS = 2
FAR = 2
PEERS = NEAR * FAR
CORES = 2
SLICE = WIDTH // PEERS
LANES = 128
HALF = 4 * RANK
ROWS = HALF * SLICE // LANES
SENT = FAR * ROWS + 8
USER_TOKENS = 8 * 256
N_DP = 32
PARTS = 8
PART = WIDTH // PARTS
RING = 8

DP = ("z", "y_hi", "core")
GROUP = ("y_mid", "y_low", "x")
VMEM = pl.BlockSpec(memory_space=pltpu.VMEM)
SMEM = pl.BlockSpec(memory_space=pltpu.SMEM)
HBM = pl.BlockSpec(memory_space=pltpu.HBM)
F32 = jnp.float32
BF16 = jnp.bfloat16
PARAMS = pltpu.CompilerParams(vmem_limit_bytes=40 * 1024 * 1024)
WIDE = pltpu.CompilerParams(vmem_limit_bytes=60 * 1024 * 1024)


def shape(*dims):
    return jax.ShapeDtypeStruct(dims, F32)


def nt(a, b):
    return lax.dot_general(a, b, (((1,), (1,)), ((), ())), preferred_element_type=F32)


def nn(a, b):
    return jnp.dot(a, b, preferred_element_type=F32)


def split(value):
    high = value.astype(BF16)
    return jnp.concatenate([high, (value - high.astype(F32)).astype(BF16)], axis=0)


def halves(value):
    return value[:RANK] + value[RANK:]


def gradient_kernel(
    x_hbm, c_hbm, adapters_hbm, user_ref, out_hbm, x_ref, c_ref, adapters_ref, out_ref, sems, out_sems
):
    copies = []
    for part in range(PARTS):
        at = pl.ds(part * PART, PART)
        copies.append(
            (
                pltpu.make_async_copy(adapters_hbm.at[:, :, :, at], adapters_ref.at[:, :, :, at], sems.at[0, part]),
                pltpu.make_async_copy(x_hbm.at[:, at], x_ref.at[:, at], sems.at[1, part]),
                pltpu.make_async_copy(c_hbm.at[:, at], c_ref.at[:, at], sems.at[2, part]),
            )
        )
    for group in copies:
        for copy in group:
            copy.start()
    from_x = jnp.zeros((2 * RANK, TOKENS), F32)
    from_c = jnp.zeros((2 * RANK, TOKENS), F32)
    mixed = jnp.zeros((RANK, RANK), F32)
    mixed_t = jnp.zeros((RANK, RANK), F32)
    for part in range(PARTS):
        for copy in copies[part]:
            copy.wait()
        at = pl.ds(part * PART, PART)
        down1, up1 = adapters_ref[0, 0, :, at], adapters_ref[0, 1, :, at]
        down2, up2 = adapters_ref[1, 0, :, at], adapters_ref[1, 1, :, at]
        from_x += nt(jnp.concatenate([down1, down2], axis=0), x_ref[:, at])
        from_c += nt(jnp.concatenate([up2, up1], axis=0), c_ref[:, at])
        mixed += nt(down2, up1)
        mixed_t += nt(up1, down2)
    z1 = from_x[:RANK].astype(BF16)
    q2 = from_c[:RANK].astype(BF16)
    z2 = (from_x[RANK:] + halves(nn(split(SCALE * mixed), z1))).astype(BF16)
    q1 = (from_c[RANK:] + halves(nn(split(SCALE * mixed_t), q2))).astype(BF16)
    cross = split((SCALE * SCALE) * nt(q2, z1))
    cross_t = split((SCALE * SCALE) * nt(z1, q2))
    left_x = jnp.concatenate([q1, q2], axis=0)
    left_c = jnp.concatenate([z1, z2], axis=0)
    sends = []
    for near in range(NEAR):
        for far in range(FAR):
            columns = pl.ds((far * NEAR + near % NEAR_YS * (NEAR // NEAR_YS) + near // NEAR_YS) * SLICE, SLICE)
            to_x = SCALE * nn(left_x, x_ref[:, columns])
            to_c = SCALE * nn(left_c, c_ref[:, columns])
            add_a2 = halves(nn(cross, adapters_ref[0, 1, :, columns]))
            add_b1 = halves(nn(cross_t, adapters_ref[1, 0, :, columns]))
            terms = (to_x[:RANK], to_c[:RANK] + add_b1, to_x[RANK:] + add_a2, to_c[RANK:])
            for half in range(SLICE // LANES):
                for k, term in enumerate(terms):
                    at = far * ROWS + half * HALF + k * RANK
                    out_ref[near, at : at + RANK, :] = term[:, half * LANES : (half + 1) * LANES]
        out_ref[near, FAR * ROWS :, :] = jnp.full((SENT - FAR * ROWS, LANES), user_ref[0].astype(F32), F32)
        send = pltpu.make_async_copy(out_ref.at[near], out_hbm.at[near], out_sems.at[near])
        send.start()
        sends.append(send)
    for send in sends:
        send.wait()


def users_kernel(mid_ref, got_ref, keep_ref, send_ref):
    mid = mid_ref[0]
    for far, out_ref in ((mid, keep_ref), (1 - mid, send_ref)):
        rows = pl.ds(pl.multiple_of(far * ROWS, ROWS), ROWS)
        sums = [jnp.zeros((ROWS, LANES), F32) for _ in range(GROUP_USERS)]
        for near in range(NEAR):
            term = got_ref[near, rows, :]
            owner = got_ref[near, FAR * ROWS : FAR * ROWS + 1, :]
            for user in range(GROUP_USERS):
                sums[user] += jnp.where(owner == float(user), term, 0.0)
        for user in range(GROUP_USERS):
            out_ref[user] = sums[user]


def squares_kernel(mid_ref, keep_ref, got_ref, sums_ref, squares_ref):
    partner = 1 - mid_ref[0]
    for user in range(GROUP_USERS):
        total = keep_ref[user] + got_ref[partner, user]
        sums_ref[user] = total
        square = jnp.sum(jnp.sum(total * total, axis=0, keepdims=True), axis=1, keepdims=True)
        squares_ref[:, user, :] = jnp.broadcast_to(square, (CORES * PEERS, LANES))


def clip_kernel(core_ref, ratio_ref, squares_ref, sums_ref, out_ref):
    rows = pl.ds(pl.multiple_of(core_ref[0] * HALF, HALF), HALF)
    bound = ratio_ref[0] * (SCALE * math.sqrt(4 * RANK * WIDTH * USER_TOKENS))
    total = jnp.zeros((HALF, LANES), F32)
    for core in range(CORES):
        squares = jnp.sum(squares_ref[core * PEERS : (core + 1) * PEERS], axis=0)
        factor = bound / jnp.maximum(jnp.sqrt(squares), bound)
        for user in range(GROUP_USERS):
            total += factor[user : user + 1] * sums_ref[core, user, rows, :]
    out_ref[...] = total


def spread_kernel(pair_ref, out_ref):
    out_ref[...] = jnp.broadcast_to((pair_ref[0] + pair_ref[1])[None], (RING, HALF, LANES))


def total_kernel(parts_ref, out_ref):
    total = parts_ref[0]
    for part in range(1, RING):
        total += parts_ref[part]
    out_ref[...] = total / (SCALE * math.sqrt(USER_TOKENS * GROUP_USERS * N_DP))


def call(kernel, out_shape, *args, scalars=0):
    several = isinstance(out_shape, tuple)
    return pl.pallas_call(
        kernel,
        out_shape=out_shape,
        in_specs=[SMEM] * scalars + [VMEM] * (len(args) - scalars),
        out_specs=(VMEM,) * len(out_shape) if several else VMEM,
        compiler_params=PARAMS,
    )(*args)


def on_device(activations, cotangent, user_ids, adapters, clip_norm_ratio):
    mid, core = lax.axis_index("y_mid")[None], lax.axis_index("core")[None]
    terms = pl.pallas_call(
        gradient_kernel,
        out_shape=shape(NEAR, SENT, LANES),
        in_specs=[HBM, HBM, HBM, SMEM],
        out_specs=HBM,
        scratch_shapes=[
            pltpu.VMEM((TOKENS, WIDTH), BF16),
            pltpu.VMEM((TOKENS, WIDTH), BF16),
            pltpu.VMEM((2, 2, RANK, WIDTH), BF16),
            pltpu.VMEM((NEAR, SENT, LANES), F32),
            pltpu.SemaphoreType.DMA((3, PARTS)),
            pltpu.SemaphoreType.DMA((NEAR,)),
        ],
        compiler_params=WIDE,
    )(activations, cotangent, adapters, user_ids)
    terms = lax.all_to_all(terms, ("x", "y_low"), 0, 0, tiled=True)
    users = shape(GROUP_USERS, ROWS, LANES)
    keep, send = call(users_kernel, (users, users), mid, terms, scalars=1)
    got = lax.all_gather(send, "y_mid")
    sums, squares = call(
        squares_kernel, (users, shape(CORES * PEERS, GROUP_USERS, LANES)), mid, keep, got, scalars=1
    )
    squares = lax.all_to_all(squares, ("core",) + GROUP, 0, 0, tiled=True)
    sums = lax.all_gather(sums, "core")
    chip = call(clip_kernel, shape(HALF, LANES), core, clip_norm_ratio, squares, sums, scalars=2)
    parts = call(spread_kernel, shape(RING, HALF, LANES), lax.all_gather(chip, "y_hi"))
    parts = lax.all_to_all(parts, "z", 0, 0, tiled=True)
    total = call(total_kernel, shape(HALF, LANES), parts)
    total = lax.all_gather(total, "core", axis=1, tiled=True)
    return total.reshape(2, 2, RANK, SLICE)


def solution(mesh):
    fine = Mesh(mesh.devices.reshape(8, 2, 2, 2, 2, 4), DP + GROUP)
    rows = P(DP + GROUP)
    return jax.shard_map(
        on_device,
        mesh=fine,
        in_specs=(rows, rows, rows, P(), P()),
        out_specs=P(None, None, None, GROUP),
        check_vma=False,
    )
```

```python
import math

import jax
import jax.numpy as jnp
from jax import lax
from jax.experimental import pallas as pl
from jax.experimental.pallas import tpu as pltpu
from jax.sharding import Mesh, PartitionSpec as P

GROUP_USERS = 2
SCALE = 2.0
RANK = 16
WIDTH = 4096
TOKENS = 256
NEAR = 8
NEAR_YS = 2
FAR = 2
PEERS = NEAR * FAR
CORES = 2
SLICE = WIDTH // PEERS
LANES = 128
HALF = 4 * RANK
ROWS = HALF * SLICE // LANES
SENT = FAR * ROWS + 8
USER_TOKENS = 8 * 256
N_DP = 32
PARTS = 8
PART = WIDTH // PARTS
RING = 8

DP = ("z", "y_hi", "core")
GROUP = ("y_mid", "y_low", "x")
VMEM = pl.BlockSpec(memory_space=pltpu.VMEM)
SMEM = pl.BlockSpec(memory_space=pltpu.SMEM)
HBM = pl.BlockSpec(memory_space=pltpu.HBM)
F32 = jnp.float32
BF16 = jnp.bfloat16
PARAMS = pltpu.CompilerParams(vmem_limit_bytes=40 * 1024 * 1024)
WIDE = pltpu.CompilerParams(vmem_limit_bytes=60 * 1024 * 1024)


def shape(*dims):
    return jax.ShapeDtypeStruct(dims, F32)


def nt(a, b):
    return lax.dot_general(a, b, (((1,), (1,)), ((), ())), preferred_element_type=F32)


def nn(a, b):
    return jnp.dot(a, b, preferred_element_type=F32)


def split(value):
    high = value.astype(BF16)
    return jnp.concatenate([high, (value - high.astype(F32)).astype(BF16)], axis=0)


def halves(value):
    return value[:RANK] + value[RANK:]


def gradient_kernel(
    x_hbm, c_hbm, adapters_hbm, user_ref, out_hbm, x_ref, c_ref, adapters_ref, out_ref, sems, out_sems
):
    copies = []
    for part in range(PARTS):
        at = pl.ds(part * PART, PART)
        copies.append(
            (
                pltpu.make_async_copy(adapters_hbm.at[:, :, :, at], adapters_ref.at[:, :, :, at], sems.at[0, part]),
                pltpu.make_async_copy(x_hbm.at[:, at], x_ref.at[:, at], sems.at[1, part]),
                pltpu.make_async_copy(c_hbm.at[:, at], c_ref.at[:, at], sems.at[2, part]),
            )
        )
    for group in copies:
        for copy in group:
            copy.start()
    from_x = jnp.zeros((2 * RANK, TOKENS), F32)
    from_c = jnp.zeros((2 * RANK, TOKENS), F32)
    mixed = jnp.zeros((RANK, RANK), F32)
    mixed_t = jnp.zeros((RANK, RANK), F32)
    for part in range(PARTS):
        for copy in copies[part]:
            copy.wait()
        at = pl.ds(part * PART, PART)
        down1, up1 = adapters_ref[0, 0, :, at], adapters_ref[0, 1, :, at]
        down2, up2 = adapters_ref[1, 0, :, at], adapters_ref[1, 1, :, at]
        from_x += nt(jnp.concatenate([down1, down2], axis=0), x_ref[:, at])
        from_c += nt(jnp.concatenate([up2, up1], axis=0), c_ref[:, at])
        mixed += nt(down2, up1)
        mixed_t += nt(up1, down2)
    z1 = from_x[:RANK].astype(BF16)
    q2 = from_c[:RANK].astype(BF16)
    z2 = (from_x[RANK:] + halves(nn(split(SCALE * mixed), z1))).astype(BF16)
    q1 = (from_c[RANK:] + halves(nn(split(SCALE * mixed_t), q2))).astype(BF16)
    cross = split((SCALE * SCALE) * nt(q2, z1))
    cross_t = split((SCALE * SCALE) * nt(z1, q2))
    left_x = jnp.concatenate([q1, q2], axis=0)
    left_c = jnp.concatenate([z1, z2], axis=0)
    sends = []
    for near in range(NEAR):
        for far in range(FAR):
            columns = pl.ds((far * NEAR + near % NEAR_YS * (NEAR // NEAR_YS) + near // NEAR_YS) * SLICE, SLICE)
            to_x = SCALE * nn(left_x, x_ref[:, columns])
            to_c = SCALE * nn(left_c, c_ref[:, columns])
            add_a2 = halves(nn(cross, adapters_ref[0, 1, :, columns]))
            add_b1 = halves(nn(cross_t, adapters_ref[1, 0, :, columns]))
            terms = (to_x[:RANK], to_c[:RANK] + add_b1, to_x[RANK:] + add_a2, to_c[RANK:])
            for half in range(SLICE // LANES):
                for k, term in enumerate(terms):
                    at = far * ROWS + half * HALF + k * RANK
                    out_ref[near, at : at + RANK, :] = term[:, half * LANES : (half + 1) * LANES]
        out_ref[near, FAR * ROWS :, :] = jnp.full((SENT - FAR * ROWS, LANES), user_ref[0].astype(F32), F32)
        send = pltpu.make_async_copy(out_ref.at[near], out_hbm.at[near], out_sems.at[near])
        send.start()
        sends.append(send)
    for send in sends:
        send.wait()


def users_kernel(mid_ref, got_ref, keep_ref, send_ref):
    mid = mid_ref[0]
    for far, out_ref in ((mid, keep_ref), (1 - mid, send_ref)):
        rows = pl.ds(pl.multiple_of(far * ROWS, ROWS), ROWS)
        sums = [jnp.zeros((ROWS, LANES), F32) for _ in range(GROUP_USERS)]
        for near in range(NEAR):
            term = got_ref[near, rows, :]
            owner = got_ref[near, FAR * ROWS : FAR * ROWS + 1, :]
            for user in range(GROUP_USERS):
                sums[user] += jnp.where(owner == float(user), term, 0.0)
        for user in range(GROUP_USERS):
            out_ref[user] = sums[user]


def squares_kernel(mid_ref, keep_ref, got_ref, sums_ref, squares_ref):
    partner = 1 - mid_ref[0]
    for user in range(GROUP_USERS):
        total = keep_ref[user] + got_ref[partner, user]
        sums_ref[user] = total
        square = jnp.sum(jnp.sum(total * total, axis=0, keepdims=True), axis=1, keepdims=True)
        squares_ref[:, user, :] = jnp.broadcast_to(square, (CORES * PEERS, LANES))


def clip_kernel(core_ref, ratio_ref, squares_ref, sums_ref, out_ref):
    rows = pl.ds(pl.multiple_of(core_ref[0] * HALF, HALF), HALF)
    bound = ratio_ref[0] * (SCALE * math.sqrt(4 * RANK * WIDTH * USER_TOKENS))
    total = jnp.zeros((HALF, LANES), F32)
    for core in range(CORES):
        squares = jnp.sum(squares_ref[core * PEERS : (core + 1) * PEERS], axis=0)
        factor = bound / jnp.maximum(jnp.sqrt(squares), bound)
        for user in range(GROUP_USERS):
            total += factor[user : user + 1] * sums_ref[core, user, rows, :]
    out_ref[...] = total


def spread_kernel(pair_ref, out_ref):
    out_ref[...] = jnp.broadcast_to((pair_ref[0] + pair_ref[1])[None], (RING, HALF, LANES))


def total_kernel(parts_ref, out_ref):
    total = parts_ref[0]
    for part in range(1, RING):
        total += parts_ref[part]
    out_ref[...] = total / (SCALE * math.sqrt(USER_TOKENS * GROUP_USERS * N_DP))


def call(kernel, out_shape, *args, scalars=0):
    several = isinstance(out_shape, tuple)
    return pl.pallas_call(
        kernel,
        out_shape=out_shape,
        in_specs=[SMEM] * scalars + [VMEM] * (len(args) - scalars),
        out_specs=(VMEM,) * len(out_shape) if several else VMEM,
        compiler_params=PARAMS,
    )(*args)


def on_device(activations, cotangent, user_ids, adapters, clip_norm_ratio):
    mid, core = lax.axis_index("y_mid")[None], lax.axis_index("core")[None]
    terms = pl.pallas_call(
        gradient_kernel,
        out_shape=shape(NEAR, SENT, LANES),
        in_specs=[HBM, HBM, HBM, SMEM],
        out_specs=HBM,
        scratch_shapes=[
            pltpu.VMEM((TOKENS, WIDTH), BF16),
            pltpu.VMEM((TOKENS, WIDTH), BF16),
            pltpu.VMEM((2, 2, RANK, WIDTH), BF16),
            pltpu.VMEM((NEAR, SENT, LANES), F32),
            pltpu.SemaphoreType.DMA((3, PARTS)),
            pltpu.SemaphoreType.DMA((NEAR,)),
        ],
        compiler_params=WIDE,
    )(activations, cotangent, adapters, user_ids)
    terms, mid, core, clip_norm_ratio = lax.optimization_barrier((terms, mid, core, clip_norm_ratio))
    terms = lax.all_to_all(terms, ("x", "y_low"), 0, 0, tiled=True)
    users = shape(GROUP_USERS, ROWS, LANES)
    keep, send = call(users_kernel, (users, users), mid, terms, scalars=1)
    got = lax.all_gather(send, "y_mid")
    sums, squares = call(
        squares_kernel, (users, shape(CORES * PEERS, GROUP_USERS, LANES)), mid, keep, got, scalars=1
    )
    squares = lax.all_to_all(squares, ("core",) + GROUP, 0, 0, tiled=True)
    sums = lax.all_gather(sums, "core")
    chip = call(clip_kernel, shape(HALF, LANES), core, clip_norm_ratio, squares, sums, scalars=2)
    parts = call(spread_kernel, shape(RING, HALF, LANES), lax.all_gather(chip, "y_hi"))
    parts = lax.all_to_all(parts, "z", 0, 0, tiled=True)
    total = call(total_kernel, shape(HALF, LANES), parts)
    total = lax.all_gather(total, "core", axis=1, tiled=True)
    return total.reshape(2, 2, RANK, SLICE)


def solution(mesh):
    fine = Mesh(mesh.devices.reshape(8, 2, 2, 2, 2, 4), DP + GROUP)
    rows = P(DP + GROUP)
    return jax.shard_map(
        on_device,
        mesh=fine,
        in_specs=(rows, rows, rows, P(), P()),
        out_specs=P(None, None, None, GROUP),
        check_vma=False,
    )
```
